32 devices in a mesh: groups: 2 (over x), mp: 16 (over z, y, core).
Axes of the slice: x: 2, y: 2, z: 4, core: 2. Of those that a mesh axis runs over, the one named last changes fastest.
Arguments:
- query_grad: bfloat16 [4096, 2048], P(('groups', 'mp')), parts along dimension 0, may hold values from -0.0029296875 to 0.0029296875
- out_basis: bfloat16 [2048, 2048], P('mp'), may hold values from -0.125 to 0.125
- in_basis: bfloat16 [2048, 2048], P('mp'), may hold values from -0.125 to 0.125
- eigen_vals: float32 [2048, 2048], P(None, 'mp'), may hold values from 0.02 to 2
- tok_inputs: bfloat16 [24576, 2048], P('mp'), may hold values from -6 to 6
- tok_grads: bfloat16 [24576, 2048], P('mp'), may hold values from -6 to 6
Outputs:
- scores: float32 [49152], P(('groups', 'mp')), parts along dimension 0
The draws below stay inside these ranges and needn't reach their ends.
There are 2 independent parts, one for each index of `groups`. The reference program is written for one: setup_inputs(seed, part) draws one part's arguments, and reference() takes and returns one part's arrays. A program takes and returns all parts, laid end to end along the dimension named above; an argument that names none is the same for every part. Nothing has to cross between parts.
All inputs are finite; a program needn't handle non-finite values.
Results may differ from the reference program's by a relative error of at most 0.0046.
Values may be sent and summed in bfloat16 or wider, within the bound.
A program may use at most 128 MiB of HBM per device.

```python
import math
import jax
import jax.numpy as jnp
from jax import lax

DO = 2048
DI = 2048
TOK_DEV = 1536
TOKENS = 24576
N_MP = 16


def levels(stream_key, dims, shards, low, high):
    gain = 1.0
    for dim, shards_of in shards:
        steps = jax.random.uniform(jax.random.fold_in(jax.random.fold_in(stream_key, 6), dim), (shards_of,), jnp.float32, low / len(shards), high / len(shards))
        gain = gain * jnp.repeat(jnp.exp(steps), dims[dim] // shards_of).reshape((-1,) + (1,) * (len(dims) - 1 - dim))
    return gain


def bell_draw(own_key, dims, scale, reach, shards=(), held_as=jnp.bfloat16):
    values = scale * jax.random.normal(own_key, dims, jnp.float32)
    if shards:
        values = values * levels(own_key, dims, shards, -0.22, 0.18)
    return jnp.clip(values, -reach, reach).astype(held_as)


def setup_inputs(seed: int = 0, part: int = 0) -> dict:
    streams_of = jax.random.split(jax.random.key(seed), 7)
    part_splits = jax.random.split(jax.random.fold_in(streams_of[6], part), 7)
    return {
        "query_grad": bell_draw(part_splits[0], (DO, DI), (DO * DI) ** -0.5, 0.0029296875, ((0, 16),)),
        "out_basis": bell_draw(streams_of[1], (DO, DO), DO ** -0.5, 0.125, ((0, 16),)),
        "in_basis": bell_draw(streams_of[2], (DI, DI), DI ** -0.5, 0.125, ((0, 16),)),
        "eigen_vals": jnp.clip(jnp.exp(math.log(2.0) - 4.6051702 * jax.random.uniform(streams_of[3], (DO, DI), jnp.float32) ** levels(streams_of[3], (DO, DI), ((1, 16),), -0.2, 0.2)), 0.02, 2.0),
        "tok_inputs": bell_draw(streams_of[4], (TOKENS, DI), 1.0, 6.0, ((0, 16),)),
        "tok_grads": bell_draw(streams_of[5], (TOKENS, DO), 1.0, 6.0, ((0, 16),)),
    }


damping = 0.05


def reference(query_grad, out_basis, in_basis, eigen_vals, tok_inputs, tok_grads):
    rotated_in = jnp.dot(query_grad, in_basis, preferred_element_type=jnp.float32).astype(jnp.bfloat16)
    rotated = jnp.dot(out_basis.T, rotated_in, preferred_element_type=jnp.float32)
    scaled = (rotated / (eigen_vals + damping)).astype(jnp.bfloat16)
    back_out = jnp.dot(out_basis, scaled, preferred_element_type=jnp.float32).astype(jnp.bfloat16)
    precond = jnp.dot(back_out, in_basis.T, preferred_element_type=jnp.float32).astype(jnp.bfloat16)
    input_blocks = tok_inputs.reshape(N_MP, TOK_DEV, DI)
    grad_blocks = tok_grads.reshape(N_MP, TOK_DEV, DO)

    def score_block(pair):
        inputs_block, grads_block = pair
        mapped = jnp.dot(inputs_block, precond.T, preferred_element_type=jnp.float32)
        return jnp.sum(grads_block.astype(jnp.float32) * mapped, axis=1)

    result = lax.map(score_block, (input_blocks, grad_blocks))
    return result.reshape(TOKENS)
```

```python
import functools

import jax
import jax.numpy as jnp
from jax import lax
from jax.experimental import pallas as pl
from jax.experimental.pallas import tpu as pltpu
from jax.sharding import PartitionSpec as P

damping = 0.05
BF, F32 = jnp.bfloat16, jnp.float32
MESH = pl.DeviceIdType.MESH


class Place:
    def __init__(self, n, groups):
        self.n, self.nz = n, n // 4
        self.me = lax.axis_index("mp")
        self.g = lax.axis_index("groups")
        self.par = lax.rem(self.g, 2)
        self.c = lax.rem(self.me, 2)
        self.y = lax.rem(self.me // 2, 2)
        self.z = self.me // 4
        self.xdev = {"groups": self.g + 1 - 2 * self.par}
        self.ydev = {"mp": self.me + 2 - 4 * self.y}
        self.cdev = {"mp": self.me + 1 - 2 * self.c}

    def block(self, z, rel_y, rel_c=0):
        y = self.y if rel_y == 0 else 1 - self.y
        c = self.c if rel_c == 0 else 1 - self.c
        return (z * 2 + y) * 2 + c


class Gather:
    def __init__(self, place, buf, rows, send, recv, share):
        self.p, self.buf, self.rows, self.send, self.recv = place, buf, rows, send, recv
        self.share = share
        self.h = (rows * 3 // 8 + 15) // 16 * 16 if share else 0

    def part(self, kind, block):
        rows, h, p = self.rows, self.h, self.p
        if kind == "all":
            start, size = block * rows, rows
        elif kind == "carried":
            start, size = block * rows + (p.par * h if h else 0), rows - h
        elif kind == "mine":
            start, size = block * rows + p.par * (rows - h), h
        else:
            start, size = block * rows + (1 - p.par) * (rows - h), h
        return self.buf.at[pl.ds(pl.multiple_of(start, 16), size), :]

    def copy(self, ref, kind, sd, rd, dev):
        return pltpu.make_async_remote_copy(
            src_ref=ref,
            dst_ref=ref,
            send_sem=self.send.at[kind, sd],
            recv_sem=self.recv.at[kind, rd],
            device_id=dev,
            device_id_type=MESH,
        )

    def sem(self, d, s):
        return d * self.p.nz + s

    def copies(self, what, d, s):
        p = self.p
        zs = p.z + s if d == 0 else p.z - s
        i = self.sem(d, s)
        if what == "z":
            nxt = p.me - 4 if d == 0 else p.me + 4
            return self.copy(
                self.part("carried", p.block(zs, 0)), 0, i, self.sem(d, s + 1), {"mp": nxt}
            )
        if what == "y":
            return self.copy(self.part("carried", p.block(zs, 0)), 1, i, i, p.ydev)
        kind, rel = what
        if kind == "x":
            return self.copy(self.part("mine", p.block(zs, rel)), 2 + rel, i, i, p.xdev)
        return self.copy(self.part("all", p.block(zs, rel)), 4 + rel, i, i, p.cdev)

    def arrived(self, what, d, s):
        p = self.p
        zs = p.z + s if d == 0 else p.z - s
        i = self.sem(d, s)
        if what == "z":
            self.copy(self.part("carried", p.block(zs, 0)), 0, i, i, p.ydev).wait_recv()
        elif what == "y":
            self.copy(self.part("carried", p.block(zs, 1)), 1, i, i, p.ydev).wait_recv()
        else:
            kind, rel = what
            if kind == "x":
                self.copy(self.part("other", p.block(zs, rel)), 2 + rel, i, i, p.xdev).wait_recv()
            else:
                ref = self.part("all", p.block(zs, rel, 1))
                self.copy(ref, 4 + rel, i, i, p.cdev).wait_recv()

    def there(self, d, s):
        return self.p.z + s < self.p.nz if d == 0 else self.p.z - s >= 0

    def onward(self, d):
        return self.p.z > 0 if d == 0 else self.p.z < self.p.nz - 1

    def each(self, s, f):
        if s == 0:
            f(0, 0)
            return
        for d in (0, 1):
            pl.when(self.there(d, s))(functools.partial(f, d, s))

    def begin(self):
        for d in (0, 1):
            pl.when(self.onward(d))(lambda d=d: self.copies("z", d, 0).start())
        self.copies("y", 0, 0).start()
        self.copies(("c", 0), 0, 0).start()

    def z_step(self, s):
        def f(d, s):
            self.arrived("z", d, s)
            if s < self.p.nz - 1:
                pl.when(self.onward(d))(lambda: self.copies("z", d, s).start())
            self.copies("y", d, s).start()
            if self.share:
                self.copies(("x", 0), d, s).start()
            else:
                self.copies(("c", 0), d, s).start()

        self.each(s, f)

    def y_step(self, s):
        def f(d, s):
            self.arrived("y", d, s)
            self.copies(("x", 1) if self.share else ("c", 1), d, s).start()

        self.each(s, f)

    def x_step(self, s):
        if not self.share:
            return

        def f(d, s):
            if s > 0:
                self.arrived(("x", 0), d, s)
                self.copies(("c", 0), d, s).start()
            self.arrived(("x", 1), d, s)
            self.copies(("c", 1), d, s).start()

        self.each(s, f)

    def c_step(self, s):
        def f(d, s):
            self.arrived(("c", 0), d, s)
            self.arrived(("c", 1), d, s)

        self.each(s, f)

    def end(self):
        for s in range(self.p.nz):

            def f(d, s):
                self.copies("y", d, s).wait_send()
                self.copies(("c", 0), d, s).wait_send()
                self.copies(("c", 1), d, s).wait_send()
                if self.share:
                    if s > 0:
                        self.copies(("x", 0), d, s).wait_send()
                    self.copies(("x", 1), d, s).wait_send()
                if 0 < s < self.p.nz - 1:
                    pl.when(self.onward(d))(lambda: self.copies("z", d, s).wait_send())

            self.each(s, f)
        for d in (0, 1):
            pl.when(self.onward(d))(lambda d=d: self.copies("z", d, 0).wait_send())


def tiles(width, f, size=512):
    @pl.loop(0, width // size)
    def _(i):
        f(pl.ds(pl.multiple_of(i * size, size), size))


def kernel(
    n, groups, q_in, uo_in, ui_in, eig_in, tok_in, grad_in, out,
    ui, uo, bt, tok, tin, acc, q, eig, m1t, xs, st,
    isend, irecv, osend, orecv, bsend, brecv, asend, arecv, local,
):
    p = Place(n, groups)
    nz, me = p.nz, p.me
    rows, width = q.shape
    do = uo.shape[1]
    tokens = tok.shape[0]
    own = pl.ds(pl.multiple_of(me * rows, rows), rows)

    loads = [
        pltpu.make_async_copy(src, dst, local.at[k])
        for k, (src, dst) in enumerate(
            [(ui_in, ui.at[own, :]), (uo_in, uo.at[own, :]), (q_in, q), (tok_in, tok), (eig_in, eig)]
        )
    ]
    for load in loads:
        load.start()

    barrier = pltpu.get_barrier_semaphore()
    for k in range(1, n):
        pl.semaphore_signal(barrier, inc=1, device_id={"mp": lax.rem(me + k, n)}, device_id_type=MESH)
    pl.semaphore_signal(barrier, inc=1, device_id=p.xdev, device_id_type=MESH)
    pl.semaphore_wait(barrier, n)

    gi = Gather(p, ui, rows, isend, irecv, True)
    go = Gather(p, uo, rows, osend, orecv, True)
    gb = Gather(p, bt, rows, bsend, brecv, False)

    loads[0].wait()
    gi.begin()
    for s in range(1, nz):
        gi.z_step(s)
        gi.y_step(s - 1)
        if s >= 2:
            gi.x_step(s - 2)
    gi.y_step(nz - 1)
    loads[1].wait()
    go.begin()
    gi.x_step(nz - 2)
    gi.x_step(nz - 1)
    for s in range(nz):
        gi.c_step(s)

    loads[2].wait()

    def first(cols):
        m1 = jnp.dot(q[...], ui[:, cols], preferred_element_type=F32)
        m1t[cols, :] = m1.T.astype(BF)

    tiles(width, first)
    xs[pl.ds(me, 1)] = m1t[own, :][None]

    def exchange(k):
        to = lax.rem(me + k, n)
        return pltpu.make_async_remote_copy(
            src_ref=m1t.at[pl.ds(pl.multiple_of(to * rows, rows), rows), :],
            dst_ref=xs.at[me],
            send_sem=asend.at[k],
            recv_sem=arecv.at[k],
            device_id={"mp": to},
            device_id_type=MESH,
        )

    def exchanged(k):
        return pltpu.make_async_remote_copy(
            src_ref=m1t.at[own, :],
            dst_ref=xs.at[lax.rem(me + n - k, n)],
            send_sem=asend.at[k],
            recv_sem=arecv.at[k],
            device_id={"mp": lax.rem(me + k, n)},
            device_id_type=MESH,
        )

    for k in range(1, n):
        exchange(k).start()

    loads[3].wait()
    piece = tokens // nz

    def rotate_tokens(s):
        r = pl.ds(s * piece, piece)

        def f(cols):
            tin[r, cols] = jnp.dot(tok[r, :], ui[:, cols], preferred_element_type=F32).astype(BF)

        tiles(width, f)

    for s in range(1, nz):
        go.z_step(s)
        go.y_step(s - 1)
        if s >= 2:
            go.x_step(s - 2)
        rotate_tokens(s - 1)
    go.y_step(nz - 1)
    go.x_step(nz - 2)
    rotate_tokens(nz - 1)
    grads = pltpu.make_async_copy(grad_in, tok, local.at[5])
    grads.start()
    go.x_step(nz - 1)
    for s in range(nz):
        go.c_step(s)
    for k in range(1, n):
        exchanged(k).wait_recv()
    loads[4].wait()

    def second(cols):
        if rows % 128 == 0:
            left = jnp.concatenate([xs[j] for j in range(n)], axis=1)
            r = jnp.dot(left, uo[:, cols], preferred_element_type=F32)
        else:
            r = jnp.zeros((rows, 512), F32)
            for j in range(n):
                r += jnp.dot(
                    xs[j], uo[pl.ds(j * rows, rows), cols], preferred_element_type=F32
                )
        st[:, cols] = (r / (eig[cols, :].T + damping)).astype(BF)

    tiles(do, second)

    def third(cols):
        b = lax.dot_general(
            st[...], uo[cols, :], (((1,), (1,)), ((), ())), preferred_element_type=F32
        )
        bt[own, cols] = b.astype(BF)

    tiles(do, third)
    gb.begin()

    step = 384 if tokens % 384 == 0 else tokens

    def add_plane(first, d, s):
        zs = p.z + s if d == 0 else p.z - s
        k = pl.ds(pl.multiple_of(zs * 4 * rows, 4 * rows), 4 * rows)

        @pl.loop(0, tokens // step)
        def _(t):
            r = pl.ds(pl.multiple_of(t * step, step), step)

            def f(cols):
                new = jnp.dot(tin_part(r, zs), bt[k, cols], preferred_element_type=F32)
                if first:
                    acc[r, cols] = new
                else:
                    acc[r, cols] += new

            tiles(do, f)

    def tin_part(r, zs):
        if 4 * rows % 128 == 0:
            return tin[r, pl.ds(pl.multiple_of(zs * 4 * rows, 4 * rows), 4 * rows)]
        raise ValueError("rows")

    for s in range(1, nz):
        gb.z_step(s)
        gb.y_step(s - 1)
        gb.c_step(s - 1)
        if s == 1:
            add_plane(True, 0, 0)
        else:
            gb.each(s - 1, functools.partial(add_plane, False))
    gb.y_step(nz - 1)
    gb.c_step(nz - 1)
    gb.each(nz - 1, functools.partial(add_plane, False))

    grads.wait()
    step2 = out.shape[1]

    @pl.loop(0, out.shape[0])
    def _(t):
        r = pl.ds(pl.multiple_of(t * step2, step2), step2)
        part = jnp.zeros((step2, 128), F32)
        for j in range(do // 128):
            cols = slice(j * 128, (j + 1) * 128)
            part += tok[r, cols].astype(F32) * acc[r, cols]
        out[pl.ds(t, 1), :] = jnp.sum(part.T, axis=0, keepdims=True)

    for g in (gi, go, gb):
        g.end()
    for k in range(1, n):
        exchange(k).wait_send()


def solution(mesh):
    n, groups = mesh.shape["mp"], mesh.shape["groups"]

    def shards(query_grad, out_basis, in_basis, eigen_vals, tok_inputs, tok_grads):
        rows, di = query_grad.shape
        do = out_basis.shape[1]
        tokens = tok_inputs.shape[0]
        nz = n // 4
        dma = pltpu.SemaphoreType.DMA
        scores = pl.pallas_call(
            functools.partial(kernel, n, groups),
            out_shape=jax.ShapeDtypeStruct((tokens // 128, 128), F32),
            in_specs=[pl.BlockSpec(memory_space=pl.ANY)] * 6,
            out_specs=pl.BlockSpec(memory_space=pltpu.VMEM),
            scratch_shapes=[
                pltpu.VMEM((di, di), BF),
                pltpu.VMEM((do, do), BF),
                pltpu.VMEM((di, do), BF),
                pltpu.VMEM((tokens, di), BF),
                pltpu.VMEM((tokens, di), BF),
                pltpu.VMEM((tokens, do), F32),
                pltpu.VMEM((rows, di), BF),
                pltpu.VMEM((do, eigen_vals.shape[1]), F32),
                pltpu.VMEM((di, rows), BF),
                pltpu.VMEM((n, rows, rows), BF),
                pltpu.VMEM((rows, do), BF),
            ]
            + [dma((6, 2 * nz))] * 6
            + [dma((n,)), dma((n,)), dma((6,))],
            compiler_params=pltpu.CompilerParams(
                collective_id=0, has_side_effects=True, vmem_limit_bytes=60 * 2**20
            ),
        )(query_grad, out_basis, in_basis, eigen_vals, tok_inputs, tok_grads)
        return scores.reshape(tokens)

    in_specs = (
        P(("groups", "mp"), None),
        P("mp", None),
        P("mp", None),
        P(None, "mp"),
        P("mp", None),
        P("mp", None),
    )
    out_specs = P(("groups", "mp"))
    return jax.shard_map(shards, mesh=mesh, in_specs=in_specs, out_specs=out_specs, check_vma=False)
```

```python
import functools

import jax
import jax.numpy as jnp
from jax import lax
from jax.experimental import pallas as pl
from jax.experimental.pallas import tpu as pltpu
from jax.sharding import PartitionSpec as P

damping = 0.05
BF, F32 = jnp.bfloat16, jnp.float32
MESH = pl.DeviceIdType.MESH
CHUNKS = 2


class Place:
    def __init__(self, n, groups):
        self.n, self.nz = n, n // 4
        self.me = lax.axis_index("mp")
        self.g = lax.axis_index("groups")
        self.par = lax.rem(self.g, 2)
        self.c = lax.rem(self.me, 2)
        self.y = lax.rem(self.me // 2, 2)
        self.z = self.me // 4
        self.xdev = {"groups": self.g + 1 - 2 * self.par}
        self.ydev = {"mp": self.me + 2 - 4 * self.y}
        self.cdev = {"mp": self.me + 1 - 2 * self.c}

    def block(self, z, rel_y, rel_c=0):
        y = self.y if rel_y == 0 else 1 - self.y
        c = self.c if rel_c == 0 else 1 - self.c
        return (z * 2 + y) * 2 + c


class Gather:
    def __init__(self, place, buf, rows, send, recv, share, chunk):
        self.p, self.buf, self.rows, self.send, self.recv = place, buf, rows, send, recv
        self.chunk = chunk
        self.width = buf.shape[1] // CHUNKS
        self.cols = pl.ds(chunk * self.width, self.width)
        self.share = share
        self.h = (rows * 3 // 8 + 15) // 16 * 16 if share else 0
        self.dup = 0

    def part(self, kind, block):
        rows, h, p = self.rows, self.h, self.p
        if kind == "all":
            start, size = block * rows, rows
        elif kind == "dup":
            start, size = block * rows, self.dup
        elif kind == "rest":
            start, size = block * rows + self.dup, rows - self.dup
        elif kind == "carried":
            start, size = block * rows + (p.par * h if h else 0), rows - h
        elif kind == "mine":
            start, size = block * rows + p.par * (rows - h), h
        else:
            start, size = block * rows + (1 - p.par) * (rows - h), h
        return self.buf.at[pl.ds(pl.multiple_of(start, 16), size), self.cols]

    def copy(self, ref, kind, sd, rd, dev):
        kind += 6 * self.chunk
        return pltpu.make_async_remote_copy(
            src_ref=ref,
            dst_ref=ref,
            send_sem=self.send.at[kind, sd],
            recv_sem=self.recv.at[kind, rd],
            device_id=dev,
            device_id_type=MESH,
        )

    def sem(self, d, s):
        return d * self.p.nz + s

    def copies(self, what, d, s):
        p = self.p
        zs = p.z + s if d == 0 else p.z - s
        i = self.sem(d, s)
        if what == "z":
            nxt = p.me - 4 if d == 0 else p.me + 4
            return self.copy(
                self.part("carried", p.block(zs, 0)), 0, i, self.sem(d, s + 1), {"mp": nxt}
            )
        if what == "dup":
            nxt = p.me - 4 if d == 0 else p.me + 4
            return self.copy(
                self.part("dup", p.block(zs, 1)), 2, i, self.sem(d, s + 1), {"mp": nxt}
            )
        if what == "y":
            kind = "rest" if self.dup and s > 0 else "carried"
            return self.copy(self.part(kind, p.block(zs, 0)), 1, i, i, p.ydev)
        kind, rel = what
        if kind == "x":
            return self.copy(self.part("mine", p.block(zs, rel)), 2 + rel, i, i, p.xdev)
        return self.copy(self.part("all", p.block(zs, rel)), 4 + rel, i, i, p.cdev)

    def arrived(self, what, d, s):
        p = self.p
        zs = p.z + s if d == 0 else p.z - s
        i = self.sem(d, s)
        if what == "z":
            self.copy(self.part("carried", p.block(zs, 0)), 0, i, i, p.ydev).wait_recv()
        elif what == "dup":
            self.copy(self.part("dup", p.block(zs, 1)), 2, i, i, p.ydev).wait_recv()
        elif what == "y":
            kind = "rest" if self.dup and s > 0 else "carried"
            self.copy(self.part(kind, p.block(zs, 1)), 1, i, i, p.ydev).wait_recv()
        else:
            kind, rel = what
            if kind == "x":
                self.copy(self.part("other", p.block(zs, rel)), 2 + rel, i, i, p.xdev).wait_recv()
            else:
                ref = self.part("all", p.block(zs, rel, 1))
                self.copy(ref, 4 + rel, i, i, p.cdev).wait_recv()

    def there(self, d, s):
        return self.p.z + s < self.p.nz if d == 0 else self.p.z - s >= 0

    def onward(self, d):
        return self.p.z > 0 if d == 0 else self.p.z < self.p.nz - 1

    def each(self, s, f):
        if s == 0:
            f(0, 0)
            return
        for d in (0, 1):
            pl.when(self.there(d, s))(functools.partial(f, d, s))

    def begin_z(self):
        for d in (0, 1):
            pl.when(self.onward(d))(lambda d=d: self.copies("z", d, 0).start())

    def begin_plane(self):
        self.copies("y", 0, 0).start()
        self.copies(("c", 0), 0, 0).start()

    def z_step(self, s):
        def f(d, s):
            self.arrived("z", d, s)
            if s < self.p.nz - 1:
                pl.when(self.onward(d))(lambda: self.copies("z", d, s).start())
            self.copies("y", d, s).start()
            if self.share:
                self.copies(("x", 0), d, s).start()
            else:
                self.copies(("c", 0), d, s).start()

        self.each(s, f)

    def y_step(self, s):
        def f(d, s):
            if self.dup and s > 0:
                self.arrived("dup", d, s)
                if s < self.p.nz - 1:
                    pl.when(self.onward(d))(lambda: self.copies("dup", d, s).start())
            self.arrived("y", d, s)
            self.copies(("x", 1) if self.share else ("c", 1), d, s).start()

        self.each(s, f)
        if self.dup and s == 0:
            for d in (0, 1):
                pl.when(self.onward(d))(lambda d=d: self.copies("dup", d, 0).start())

    def x_step(self, s):
        if not self.share:
            return

        def f(d, s):
            if s > 0:
                self.arrived(("x", 0), d, s)
                self.copies(("c", 0), d, s).start()
            self.arrived(("x", 1), d, s)
            self.copies(("c", 1), d, s).start()

        self.each(s, f)

    def c_step(self, s):
        def f(d, s):
            self.arrived(("c", 0), d, s)
            self.arrived(("c", 1), d, s)

        self.each(s, f)

    def end(self):
        for s in range(self.p.nz):

            def f(d, s):
                self.copies("y", d, s).wait_send()
                self.copies(("c", 0), d, s).wait_send()
                self.copies(("c", 1), d, s).wait_send()
                if self.share:
                    if s > 0:
                        self.copies(("x", 0), d, s).wait_send()
                    self.copies(("x", 1), d, s).wait_send()
                if 0 < s < self.p.nz - 1:
                    pl.when(self.onward(d))(lambda: self.copies("z", d, s).wait_send())
                    if self.dup:
                        pl.when(self.onward(d))(lambda: self.copies("dup", d, s).wait_send())

            self.each(s, f)
        for d in (0, 1):
            pl.when(self.onward(d))(lambda d=d: self.copies("z", d, 0).wait_send())
            if self.dup:
                pl.when(self.onward(d))(lambda d=d: self.copies("dup", d, 0).wait_send())


def tiles(width, f, size=512, start=0):
    @pl.loop(0, width // size)
    def _(i):
        f(pl.ds(pl.multiple_of(start + i * size, size), size))


def kernel(
    n, groups, q_in, uo_in, ui_in, eig_in, tok_in, grad_in, out,
    ui, uo, bt, tok, tin, acc, parts, q, eig, m1t, xs, st,
    isend, irecv, osend, orecv, bsend, brecv, asend, arecv, local,
):
    p = Place(n, groups)
    nz, me = p.nz, p.me
    rows, width = q.shape
    do = uo.shape[1]
    tokens = tok.shape[0]
    own = pl.ds(pl.multiple_of(me * rows, rows), rows)

    loads = [
        pltpu.make_async_copy(src, dst, local.at[k])
        for k, (src, dst) in enumerate(
            [(ui_in, ui.at[own, :]), (uo_in, uo.at[own, :]), (q_in, q), (tok_in, tok), (eig_in, eig)]
        )
    ]
    for load in loads:
        load.start()

    barrier = pltpu.get_barrier_semaphore()
    for k in range(1, n):
        pl.semaphore_signal(barrier, inc=1, device_id={"mp": lax.rem(me + k, n)}, device_id_type=MESH)
    pl.semaphore_signal(barrier, inc=1, device_id=p.xdev, device_id_type=MESH)
    pl.semaphore_wait(barrier, n)

    gi = [Gather(p, ui, rows, isend, irecv, True, h) for h in range(CHUNKS)]
    go = [Gather(p, uo, rows, osend, orecv, True, h) for h in range(CHUNKS)]
    gb = [Gather(p, bt, rows, bsend, brecv, False, h) for h in range(CHUNKS)]

    loads[0].wait()
    for g in gi:
        g.begin_z()
        g.begin_plane()
    for s in range(1, nz):
        for g in gi:
            g.z_step(s)
            g.y_step(s - 1)
        if s >= 2:
            for g in gi:
                g.x_step(s - 2)
    loads[1].wait()
    for g in go:
        g.begin_z()
    for g in gi:
        g.y_step(nz - 1)
        g.x_step(nz - 2)
    for g in go:
        g.begin_plane()
    for g in go:
        g.z_step(1)

    loads[2].wait()

    def first(cols):
        m1 = jnp.dot(q[...], ui[:, cols], preferred_element_type=F32)
        m1t[cols, :] = m1.T.astype(BF)

    def exchange(k):
        to = lax.rem(me + k, n)
        return pltpu.make_async_remote_copy(
            src_ref=m1t.at[pl.ds(pl.multiple_of(to * rows, rows), rows), :],
            dst_ref=xs.at[me],
            send_sem=asend.at[k],
            recv_sem=arecv.at[k],
            device_id={"mp": to},
            device_id_type=MESH,
        )

    def exchanged(k):
        return pltpu.make_async_remote_copy(
            src_ref=m1t.at[own, :],
            dst_ref=xs.at[lax.rem(me + n - k, n)],
            send_sem=asend.at[k],
            recv_sem=arecv.at[k],
            device_id={"mp": lax.rem(me + k, n)},
            device_id_type=MESH,
        )

    for g in gi:
        g.x_step(nz - 1)
        for s in range(nz):
            g.c_step(s)
        tiles(g.width, first, start=g.chunk * g.width)
        for k in range(1, n):
            now = lax.rem(me + k, n) // (n // CHUNKS) == g.chunk
            pl.when(now)(lambda k=k: exchange(k).start())
    xs[pl.ds(me, 1)] = m1t[own, :][None]

    loads[3].wait()
    piece = tokens // nz

    def rotate_tokens(s):
        r = pl.ds(s * piece, piece)

        def f(cols):
            tin[r, cols] = jnp.dot(tok[r, :], ui[:, cols], preferred_element_type=F32).astype(BF)

        tiles(width, f)

    for s in range(1, nz):
        for g in go:
            if s > 1:
                g.z_step(s)
            g.y_step(s - 1)
        if s >= 2:
            for g in go:
                g.x_step(s - 2)
        rotate_tokens(s - 1)
    for g in go:
        g.y_step(nz - 1)
        g.x_step(nz - 2)
    rotate_tokens(nz - 1)
    grads = pltpu.make_async_copy(grad_in, tok, local.at[5])
    grads.start()
    for g in go:
        g.x_step(nz - 1)
        for s in range(nz):
            g.c_step(s)
    for k in range(1, n):
        exchanged(k).wait_recv()
    loads[4].wait()

    def second(cols):
        if rows % 128 == 0:
            left = jnp.concatenate([xs[j] for j in range(n)], axis=1)
            r = jnp.dot(left, uo[:, cols], preferred_element_type=F32)
        else:
            r = jnp.zeros((rows, 512), F32)
            for j in range(n):
                r += jnp.dot(
                    xs[j], uo[pl.ds(j * rows, rows), cols], preferred_element_type=F32
                )
        st[:, cols] = (r / (eig[cols, :].T + damping)).astype(BF)

    tiles(do, second)

    def third(cols):
        b = lax.dot_general(
            st[...], uo[cols, :], (((1,), (1,)), ((), ())), preferred_element_type=F32
        )
        bt[own, cols] = b.astype(BF)

    for g in gb:
        tiles(g.width, third, start=g.chunk * g.width)
        g.begin_z()
        g.begin_plane()

    step = 384 if tokens % 384 == 0 else tokens

    def add_plane(g, first, d, s):
        zs = p.z + s if d == 0 else p.z - s
        k = pl.ds(pl.multiple_of(zs * 4 * rows, 4 * rows), 4 * rows)

        @pl.loop(0, tokens // step)
        def _(t):
            r = pl.ds(pl.multiple_of(t * step, step), step)

            def f(cols):
                new = jnp.dot(tin[r, k], bt[k, cols], preferred_element_type=F32)
                if first:
                    acc[r, cols] = new
                else:
                    acc[r, cols] += new

            tiles(g.width, f, start=g.chunk * g.width)

    def add_scores(g):
        @pl.loop(0, out.shape[0])
        def _(t):
            r = pl.ds(pl.multiple_of(t * 128, 128), 128)
            part = jnp.zeros((128, 128), F32) if g.chunk == 0 else parts[r, :]
            for j in range(g.width // 128):
                cols = slice(g.chunk * g.width + j * 128, g.chunk * g.width + (j + 1) * 128)
                part += tok[r, cols].astype(F32) * acc[r, cols]
            if g.chunk == CHUNKS - 1:
                out[pl.ds(t, 1), :] = jnp.sum(part.T, axis=0, keepdims=True)
            else:
                parts[r, :] = part

    for s in range(1, nz):
        for g in gb:
            g.z_step(s)
            g.y_step(s - 1)
        for g in gb:
            g.c_step(s - 1)
            if s == 1:
                add_plane(g, True, 0, 0)
            else:
                g.each(s - 1, functools.partial(add_plane, g, False))
    for g in gb:
        g.y_step(nz - 1)
    grads.wait()
    for g in gb:
        g.c_step(nz - 1)
        g.each(nz - 1, functools.partial(add_plane, g, False))
        add_scores(g)

    for g in gi + go + gb:
        g.end()
    for k in range(1, n):
        exchange(k).wait_send()


def solution(mesh):
    n, groups = mesh.shape["mp"], mesh.shape["groups"]

    def shards(query_grad, out_basis, in_basis, eigen_vals, tok_inputs, tok_grads):
        rows, di = query_grad.shape
        do = out_basis.shape[1]
        tokens = tok_inputs.shape[0]
        nz = n // 4
        dma = pltpu.SemaphoreType.DMA
        scores = pl.pallas_call(
            functools.partial(kernel, n, groups),
            out_shape=jax.ShapeDtypeStruct((tokens // 128, 128), F32),
            in_specs=[pl.BlockSpec(memory_space=pl.ANY)] * 6,
            out_specs=pl.BlockSpec(memory_space=pltpu.VMEM),
            scratch_shapes=[
                pltpu.VMEM((di, di), BF),
                pltpu.VMEM((do, do), BF),
                pltpu.VMEM((di, do), BF),
                pltpu.VMEM((tokens, di), BF),
                pltpu.VMEM((tokens, di), BF),
                pltpu.VMEM((tokens, do), F32),
                pltpu.VMEM((tokens, 128), F32),
                pltpu.VMEM((rows, di), BF),
                pltpu.VMEM((do, eigen_vals.shape[1]), F32),
                pltpu.VMEM((di, rows), BF),
                pltpu.VMEM((n, rows, rows), BF),
                pltpu.VMEM((rows, do), BF),
            ]
            + [dma((6 * CHUNKS, 2 * nz))] * 6
            + [dma((n,)), dma((n,)), dma((6,))],
            compiler_params=pltpu.CompilerParams(
                collective_id=0, has_side_effects=True, vmem_limit_bytes=60 * 2**20
            ),
        )(query_grad, out_basis, in_basis, eigen_vals, tok_inputs, tok_grads)
        return scores.reshape(tokens)

    in_specs = (
        P(("groups", "mp"), None),
        P("mp", None),
        P("mp", None),
        P(None, "mp"),
        P("mp", None),
        P("mp", None),
    )
    out_specs = P(("groups", "mp"))
    return jax.shard_map(shards, mesh=mesh, in_specs=in_specs, out_specs=out_specs, check_vma=False)
```
